32 devices in a mesh: dp: 4 (over x, core), fsdp: 4 (over z), seq: 2 (over y).
Axes of the slice: x: 2, y: 2, z: 4, core: 2. Of those that a mesh axis runs over, the one named last changes fastest.
Arguments:
- frames: bfloat16 [16, 512, 1536], P(('dp', 'fsdp'), 'seq'), may hold values from -6 to 6
- projection: bfloat16 [1536, 3072], P('fsdp'), may hold values from -1 to 1
- lengths: int32 [16], P(('dp', 'fsdp')), may hold values from 128 to 512
- cotangent: bfloat16 [16, 512, 1024], P(('dp', 'fsdp'), 'seq'), may hold values from -24 to 24
Outputs:
- context: bfloat16 [16, 512, 1024], P(('dp', 'fsdp'), 'seq')
- input_gradient: float32 [16, 512, 1536], P(('dp', 'fsdp'), 'seq')
- projection_gradient: float32 [1536, 3072], P(('dp', 'fsdp', 'seq'))
The draws below stay inside these ranges and needn't reach their ends.
All inputs are finite; a program needn't handle non-finite values.
Results may differ from the reference program's by a relative error of at most 0.007.
The reference program's roundings to bfloat16 on the way (of `normed`, `packed`, `weights`, `masked`, `value_gradient`, `score_gradient`, `query_gradient` and `key_gradient`) count: a program that leaves them out, or rounds other values in their place, can miss the bound.
Values may be sent and summed in bfloat16 or wider, within the bound.
A program may use at most 128 MiB of HBM per device.

```python
import math
import jax
import jax.numpy as jnp
from jax import lax

D = 1536
HEADS = 16
HD = 64
FRAMES = 512
RECS = 16


def draw_frames(key, part):
    base = jax.random.normal(jax.random.fold_in(key, 1), (RECS, FRAMES, D), jnp.float32)
    return jnp.clip(base, -6.0, 6.0).astype(jnp.bfloat16)


def draw_projection(key, part):
    base = jax.random.normal(jax.random.fold_in(key, 11), (D, 3, HEADS, HD), jnp.float32) / math.sqrt(D)
    return jnp.clip(base, -1.0, 1.0).reshape(D, 3 * HEADS * HD).astype(jnp.bfloat16)


def draw_cotangent(key, part):
    base = jax.random.normal(jax.random.fold_in(key, 21), (RECS, FRAMES, HEADS * HD), jnp.float32)
    return jnp.clip(4.0 * base, -24.0, 24.0).astype(jnp.bfloat16)


def set_ends(values, key, smallest, largest):
    dims = values.shape
    spot = [jax.random.randint(jax.random.fold_in(key, axis), (), 0, dims[axis]) for axis in range(len(dims))]
    values = values.at[tuple(spot)].set(smallest)
    longest = dims.index(max(dims))
    spot[longest] = (spot[longest] + 1) % dims[longest]
    return values.at[tuple(spot)].set(largest)


def setup_inputs(seed: int = 0) -> dict:
    splits = jax.random.split(jax.random.key(seed), 5)
    return {
        "frames": draw_frames(jax.random.fold_in(splits[4], 71), 0),
        "projection": draw_projection(jax.random.fold_in(splits[4], 71), 0),
        "lengths": set_ends(jax.random.randint(splits[2], (RECS,), FRAMES // 4, FRAMES + 1), jax.random.fold_in(splits[2], 1), FRAMES // 4, FRAMES).astype(jnp.int32),
        "cotangent": draw_cotangent(jax.random.fold_in(splits[4], 71), 0),
    }


EPS = 1e-05

def attend_rows(query_rows, key_rows, valid):
    factor = 1.0 / math.sqrt(HD)
    scores = jnp.einsum('qhd,khd->hqk', query_rows.astype(jnp.float32), key_rows.astype(jnp.float32)) * factor
    scores = jnp.where(valid[None, None, :], scores, -jnp.inf)
    row_peak = lax.optimization_barrier(jnp.max(scores, axis=2, keepdims=True))
    exponentials = jnp.exp(scores - row_peak)
    return exponentials / lax.optimization_barrier(jnp.sum(exponentials, axis=2, keepdims=True))

def reference(frames, projection, lengths, cotangent):
    feature_width = HEADS * HD
    factor = 1.0 / math.sqrt(HD)

    def one_recording(running, inputs):
        rows_in, length, upstream = inputs
        as_float = rows_in.astype(jnp.float32)
        centered = as_float - lax.optimization_barrier(jnp.mean(as_float, axis=1, keepdims=True))
        inv_std = lax.rsqrt(lax.optimization_barrier(jnp.mean(centered * centered, axis=1, keepdims=True)) + EPS)
        standard = centered * inv_std
        normed = standard.astype(jnp.bfloat16)
        packed = jnp.dot(normed, projection, preferred_element_type=jnp.float32).astype(jnp.bfloat16)
        packed = packed.reshape(FRAMES, 3, HEADS, HD)
        query_rows = packed[:, 0]
        key_rows = packed[:, 1]
        value_rows = packed[:, 2]
        valid = jnp.arange(FRAMES, dtype=jnp.int32) < length
        probabilities = attend_rows(query_rows, key_rows, valid)
        weights = probabilities.astype(jnp.bfloat16)
        mixture = jnp.einsum('hqk,khd->qhd', weights.astype(jnp.float32), value_rows.astype(jnp.float32))
        mixture = jnp.where(valid[:, None, None], mixture, jnp.zeros_like(mixture)).astype(jnp.bfloat16)
        masked = jnp.where(valid[:, None], upstream, jnp.zeros_like(upstream)).reshape(FRAMES, HEADS, HD)
        value_gradient = jnp.einsum('hqk,qhd->khd', weights.astype(jnp.float32), masked.astype(jnp.float32)).astype(jnp.bfloat16)
        prob_gradient = jnp.einsum('qhd,khd->hqk', masked.astype(jnp.float32), value_rows.astype(jnp.float32))
        row_inner = lax.optimization_barrier(jnp.sum(probabilities * prob_gradient, axis=2, keepdims=True))
        score_gradient = (probabilities * (prob_gradient - row_inner) * factor).astype(jnp.bfloat16)
        query_gradient = jnp.einsum('hqk,khd->qhd', score_gradient.astype(jnp.float32), key_rows.astype(jnp.float32)).astype(jnp.bfloat16)
        key_gradient = jnp.einsum('hqk,qhd->khd', score_gradient.astype(jnp.float32), query_rows.astype(jnp.float32)).astype(jnp.bfloat16)
        packed_gradient = jnp.stack([query_gradient, key_gradient, value_gradient], axis=1).reshape(FRAMES, 3 * feature_width)
        normed_gradient = lax.dot_general(packed_gradient, projection, (((1,), (1,)), ((), ())), preferred_element_type=jnp.float32)
        row_mean = lax.optimization_barrier(jnp.mean(normed_gradient, axis=1, keepdims=True))
        projected = lax.optimization_barrier(jnp.mean(normed_gradient * standard, axis=1, keepdims=True))
        input_gradient = inv_std * (normed_gradient - row_mean - standard * projected)
        running = running + lax.dot_general(normed, packed_gradient, (((0,), (0,)), ((), ())), preferred_element_type=jnp.float32)
        return (running, (mixture.reshape(FRAMES, feature_width), input_gradient))
    start_sum = jnp.zeros((D, 3 * feature_width), jnp.float32)
    projection_gradient, outputs = lax.scan(one_recording, start_sum, (frames, lengths, cotangent))
    context, input_gradient = outputs
    return (context, input_gradient, projection_gradient)
```

```python
import functools
import math

import jax
import jax.numpy as jnp
from jax import lax
from jax.experimental import pallas as pl
from jax.experimental.pallas import tpu as pltpu
from jax.sharding import PartitionSpec as P

HEADS = 16
HD = 64
EPS = 1e-05
MESH = pl.DeviceIdType.MESH
F32 = jnp.float32
BF16 = jnp.bfloat16
VMEM_BYTES = 56 * 1024 * 1024


def ring(axis, step):
    size = lax.axis_size(axis)
    return lax.rem(lax.axis_index(axis) + step + size, size)


def greet(seq_count, fsdp_count, dp):
    barrier = pltpu.get_barrier_semaphore()
    for peer in (dp ^ 1, dp ^ 2):
        pl.semaphore_signal(barrier, inc=1, device_id={"dp": peer}, device_id_type=MESH)
    for d in range(1, fsdp_count):
        pl.semaphore_signal(barrier, inc=1, device_id={"fsdp": ring("fsdp", d)}, device_id_type=MESH)
    for d in range(1, seq_count):
        pl.semaphore_signal(barrier, inc=1, device_id={"seq": ring("seq", d)}, device_id_type=MESH)
    pl.semaphore_wait(barrier, 2 + fsdp_count - 1 + seq_count - 1)


def gather_kernel(
    seq_count, fsdp_count, w_ref, x_ref, c_ref, w_all, x_all, c_all,
    local_sem, xs, xr, cs, cr, zs, zr, f1s, f1r, f2s, f2r, f3s, f3r,
):
    dp = lax.axis_index("dp")
    fs = lax.axis_index("fsdp")
    me = lax.axis_index("seq")
    rows = w_ref.shape[0]
    quarter = rows // 4
    local = x_ref.shape[0]
    gw = c_all.shape[1]
    greet(seq_count, fsdp_count, dp)

    def part(block, q):
        return w_all.at[pl.ds(pl.multiple_of(block * rows + q * quarter, 16), quarter)]

    def remote(src, dst, send, recv, where):
        return pltpu.make_async_remote_copy(
            src_ref=src, dst_ref=dst, send_sem=send, recv_sem=recv, device_id=where, device_id_type=MESH
        )

    sent = []
    z_copies = {}
    for d in range(1, fsdp_count):
        copy = remote(
            w_ref.at[pl.ds(pl.multiple_of(dp * quarter, 16), quarter)],
            part(fs, dp), zs.at[d], zr.at[d], {"fsdp": ring("fsdp", d)},
        )
        copy.start()
        z_copies[d] = copy
        sent.append(copy)
    here = pl.ds(pl.multiple_of(me * local, 16), local)
    seq_copies = []
    for d in range(1, seq_count):
        peer = ring("seq", d)
        a = remote(x_ref, x_all.at[here], xs.at[d], xr.at[d], {"seq": peer})
        b = remote(
            c_ref.at[:, pl.ds(pl.multiple_of(peer * gw, 128), gw)],
            c_all.at[here], cs.at[d], cr.at[d], {"seq": peer},
        )
        a.start()
        b.start()
        seq_copies += [a, b]
    mine = [
        pltpu.make_async_copy(w_ref, w_all.at[pl.ds(pl.multiple_of(fs * rows, 16), rows)], local_sem.at[0]),
        pltpu.make_async_copy(x_ref, x_all.at[here], local_sem.at[1]),
        pltpu.make_async_copy(
            c_ref.at[:, pl.ds(pl.multiple_of(me * gw, 128), gw)], c_all.at[here], local_sem.at[2]
        ),
    ]
    for copy in mine:
        copy.start()
    order = sorted(range(1, fsdp_count), key=lambda d: min(d, fsdp_count - d))
    first, second, third = {}, {}, {}
    for d in order:
        z_copies[d].wait_recv()
        block = ring("fsdp", -d)
        second[d] = remote(part(block, dp), part(block, dp), f2s.at[d], f2r.at[d], {"dp": dp ^ 2})
        second[d].start()
        first[d] = remote(part(block, dp), part(block, dp), f1s.at[d], f1r.at[d], {"dp": dp ^ 1})
        first[d].start()
    for d in order:
        second[d].wait_recv()
        block = ring("fsdp", -d)
        third[d] = remote(part(block, dp ^ 2), part(block, dp ^ 2), f3s.at[d], f3r.at[d], {"dp": dp ^ 1})
        third[d].start()
    for d in order:
        first[d].wait_recv()
        third[d].wait_recv()
    for copy in seq_copies:
        copy.wait_recv()
    for copy in mine:
        copy.wait()
    for copy in sent + seq_copies:
        copy.wait_send()
    for d in order:
        first[d].wait_send()
        second[d].wait_send()
        third[d].wait_send()


def gather(w_mine, x, c, seq_count, fsdp_count, gw):
    any_spec = pl.BlockSpec(memory_space=pl.ANY)
    dma = pltpu.SemaphoreType.DMA
    total = x.shape[0] * seq_count
    return pl.pallas_call(
        functools.partial(gather_kernel, seq_count, fsdp_count),
        out_shape=(
            jax.ShapeDtypeStruct((w_mine.shape[0] * fsdp_count, w_mine.shape[1]), BF16),
            jax.ShapeDtypeStruct((total, x.shape[1]), BF16),
            jax.ShapeDtypeStruct((total, gw), BF16),
        ),
        in_specs=[any_spec] * 3,
        out_specs=(any_spec,) * 3,
        scratch_shapes=[dma((3,))] + [dma((seq_count,))] * 4 + [dma((fsdp_count,))] * 8,
        compiler_params=pltpu.CompilerParams(collective_id=0, has_side_effects=True),
        name="gather_inputs",
    )(w_mine, x, c)


def nt(a, b):
    return lax.dot_general(a, b, (((1,), (1,)), ((), ())), preferred_element_type=F32)


def tn(a, b):
    return lax.dot_general(a, b, (((0,), (0,)), ((), ())), preferred_element_type=F32)


def attention_kernel(len_ref, q_ref, k_ref, v_ref, o_ref, ctx_ref, grad_ref, dk_acc, dv_acc):
    pair = pl.program_id(0)
    step = pl.program_id(1)
    steps = pl.num_programs(1)
    length = len_ref[0]
    block, width = q_ref.shape
    keys = k_ref.shape[0]
    gw = grad_ref.shape[1] // 3
    factor = 1.0 / math.sqrt(HD)
    key_ok = lax.broadcasted_iota(jnp.int32, (keys, block), 0) < length
    row = lax.broadcasted_iota(jnp.int32, (block, width), 0) + step * block
    row_ok = row < length
    k, v, q = k_ref[...], v_ref[...], q_ref[...]
    upstream = jnp.where(row_ok, o_ref[...], jnp.zeros_like(o_ref[...]))
    key_lane = lax.broadcasted_iota(jnp.int32, (keys, width), 1)
    row_lane = lax.broadcasted_iota(jnp.int32, (block, width), 1)

    @pl.when(step == 0)
    def _():
        dk_acc[...] = jnp.zeros_like(dk_acc)
        dv_acc[...] = jnp.zeros_like(dv_acc)

    context_t = jnp.zeros((width, block), F32)
    query_t = jnp.zeros((width, block), F32)
    dk = dk_acc[...]
    dv = dv_acc[...]
    for head in range(width // HD):
        low, high = head * HD, (head + 1) * HD
        on_key = (key_lane >= low) & (key_lane < high)
        on_row = (row_lane >= low) & (row_lane < high)
        k_h = jnp.where(on_key, k, jnp.zeros_like(k))
        v_h = jnp.where(on_key, v, jnp.zeros_like(v))
        q_h = jnp.where(on_row, q, jnp.zeros_like(q))
        o_h = jnp.where(on_row, upstream, jnp.zeros_like(upstream))
        scores = jnp.where(key_ok, nt(k_h, q), -jnp.inf)
        peak = jnp.max(scores, axis=0, keepdims=True)
        e = jnp.exp((scores - peak) * factor)
        p = e * (1.0 / jnp.sum(e, axis=0, keepdims=True))
        weights = p.astype(BF16)
        context_t += tn(v_h, weights)
        dv += jnp.dot(weights, o_h, preferred_element_type=F32)
        dp = nt(v_h, upstream)
        inner = jnp.sum(p * dp, axis=0, keepdims=True)
        ds = (p * (dp - inner) * factor).astype(BF16)
        query_t += tn(k_h, ds)
        dk += jnp.dot(ds, q_h, preferred_element_type=F32)
    context = context_t.T
    ctx_ref[...] = jnp.where(row_ok, context, jnp.zeros_like(context)).astype(BF16)
    rows = pl.ds(pl.multiple_of(step * block, block), block)
    column = pl.multiple_of(pair * width, width)
    grad_ref[rows, pl.ds(column, width)] = query_t.T.astype(BF16)
    dk_acc[...] = dk
    dv_acc[...] = dv

    @pl.when(step == steps - 1)
    def _():
        grad_ref[:, pl.ds(pl.multiple_of(gw + column, width), width)] = dk.astype(BF16)
        grad_ref[:, pl.ds(pl.multiple_of(2 * gw + column, width), width)] = dv.astype(BF16)


def attention(length, packed, c_all, gw):
    total = packed.shape[0]
    block = min(total, 512)
    width = 2 * HD
    pairs = gw // width
    return pl.pallas_call(
        attention_kernel,
        grid=(pairs, total // block),
        out_shape=(
            jax.ShapeDtypeStruct((total, gw), BF16),
            jax.ShapeDtypeStruct((total, 3 * gw), BF16),
        ),
        in_specs=[
            pl.BlockSpec(memory_space=pltpu.SMEM),
            pl.BlockSpec((block, width), lambda h, i: (i, h)),
            pl.BlockSpec((total, width), lambda h, i: (0, pairs + h)),
            pl.BlockSpec((total, width), lambda h, i: (0, 2 * pairs + h)),
            pl.BlockSpec((block, width), lambda h, i: (i, h)),
        ],
        out_specs=(
            pl.BlockSpec((block, width), lambda h, i: (i, h)),
            pl.BlockSpec((total, 3 * gw), lambda h, i: (0, 0)),
        ),
        scratch_shapes=[pltpu.VMEM((total, width), F32)] * 2,
        compiler_params=pltpu.CompilerParams(vmem_limit_bytes=VMEM_BYTES),
        cost_estimate=pl.CostEstimate(
            flops=12 * total * total * gw, bytes_accessed=16 * total * gw, transcendentals=total * total * gw // HD
        ),
        name="attention",
    )(length, packed, packed, packed, c_all)


def encode(value):
    peak = jnp.maximum(jnp.max(jnp.abs(value), axis=0, keepdims=True), 1e-30)
    code = jnp.round(value * (32767.0 / peak)).astype(jnp.int32).astype(jnp.int16)
    return code, peak * (1.0 / 32767.0)


def decode(code, scale):
    return code.astype(jnp.int32).astype(F32) * scale


def reduce_kernel(
    seq_count, fsdp_count, nt_ref, grad_ref, dx_ref, ctx_ref, out_ref, dx_out, ctx_out,
    s1, r1, s2, r2, t2, u2, s3, r3, t3, u3, total, s4,
    local_sem, s1s, s1r, s2s, s2r, t2s, t2r, s3s, s3r, t3s, t3r, s4s, s4r, xs, xr, cs, cr,
):
    dp = lax.axis_index("dp")
    fs = lax.axis_index("fsdp")
    me = lax.axis_index("seq")
    features = nt_ref.shape[0]
    rows = features // (4 * fsdp_count)
    local = dx_out.shape[1]
    gw = ctx_ref.shape[1]
    final = rows // seq_count
    greet(seq_count, fsdp_count, dp)

    def remote(src, dst, send, recv, where):
        return pltpu.make_async_remote_copy(
            src_ref=src, dst_ref=dst, send_sem=send, recv_sem=recv, device_id=where, device_id_type=MESH
        )

    mine_columns = pl.ds(pl.multiple_of(me * gw, 128), gw)
    seq_copies = []
    for d in range(1, seq_count):
        peer = ring("seq", d)
        there = pl.ds(pl.multiple_of(peer * local, 16), local)
        a = remote(dx_ref.at[there], dx_out.at[d - 1], xs.at[d], xr.at[d], {"seq": peer})
        b = remote(ctx_ref.at[there], ctx_out.at[:, mine_columns], cs.at[d], cr.at[d], {"seq": peer})
        seq_copies += [a, b]
    own = pltpu.make_async_copy(
        ctx_ref.at[pl.ds(pl.multiple_of(me * local, 16), local)], ctx_out.at[:, mine_columns], local_sem
    )
    for copy in seq_copies:
        copy.start()
    own.start()

    def product(block, step):
        sub = lax.rem(fs + 1 + step, fsdp_count)
        start = pl.multiple_of(block * (rows * fsdp_count) + sub * rows, 16)
        return jnp.dot(nt_ref[pl.ds(start, rows), :], grad_ref[...], preferred_element_type=F32)

    core = lax.rem(dp, 2)
    far = 2 * (1 - dp // 2)
    near = 2 * (dp // 2)

    def copy1(i):
        return remote(s1.at[i], r1.at[i], s1s.at[i], s1r.at[i], {"dp": dp ^ 1})

    def copy2(d):
        return (
            remote(s2.at[d], r2.at[d], s2s.at[d], s2r.at[d], {"dp": dp ^ 2}),
            remote(t2.at[d], u2.at[d], t2s.at[d], t2r.at[d], {"dp": dp ^ 2}),
        )

    def copy3(d):
        peer = lax.rem(fs + 1 + d, fsdp_count)
        return (
            remote(s3.at[d], r3.at[d], s3s.at[d], s3r.at[d], {"fsdp": peer}),
            remote(t3.at[d], u3.at[d], t3s.at[d], t3r.at[d], {"fsdp": peer}),
        )

    def loop(count, body):
        lax.fori_loop(0, count, lambda i, _: (body(i), 0)[1], 0)

    def to_core(i):
        block = jnp.where(i < fsdp_count, far, near) + (1 - core)
        s1[i] = product(block, lax.rem(i, fsdp_count))
        copy1(i).start()

    loop(2 * fsdp_count, to_core)

    def to_x(d):
        own_part = product(far + core, d)
        copy1(d).wait_recv()
        code, scale = encode(own_part + r1[d])
        s2[d] = code
        t2[d] = scale
        for copy in copy2(d):
            copy.start()

    loop(fsdp_count, to_x)

    def arrived(d):
        own_part = product(near + core, d)
        copy1(fsdp_count + d).wait_recv()
        for copy in copy2(d):
            copy.wait_recv()
        return own_part + r1[fsdp_count + d] + decode(r2[d], u2[d])

    def to_z(d):
        code, scale = encode(arrived(d))
        s3[d] = code
        t3[d] = scale
        for copy in copy3(d):
            copy.start()

    loop(fsdp_count - 1, to_z)
    total[...] = arrived(fsdp_count - 1)

    def add_z(d):
        for copy in copy3(d):
            copy.wait_recv()
        total[...] += decode(r3[d], u3[d])

    loop(fsdp_count - 1, add_z)
    for p in range(seq_count):
        s4[p] = total[p * final : (p + 1) * final, :]
    last = []
    for d in range(1, seq_count):
        peer = ring("seq", d)
        copy = remote(s4.at[peer], out_ref.at[me], s4s.at[d], s4r.at[d], {"seq": peer})
        copy.start()
        last.append(copy)
    out_ref[me] = s4[me]
    for copy in last:
        copy.wait()
    for copy in seq_copies:
        copy.wait()
    own.wait()

    def drain1(i):
        copy1(i).wait_send()

    def drain2(d):
        for copy in copy2(d):
            copy.wait_send()

    def drain3(d):
        for copy in copy3(d):
            copy.wait_send()

    loop(2 * fsdp_count, drain1)
    loop(fsdp_count, drain2)
    loop(fsdp_count - 1, drain3)


def reduce(normed_t, grad, dx, ctx, seq_count, fsdp_count, local):
    features, columns = normed_t.shape[0], grad.shape[1]
    gw = columns // 3
    rows = features // (4 * fsdp_count)
    final = rows // seq_count
    vmem = pl.BlockSpec(memory_space=pltpu.VMEM)
    any_spec = pl.BlockSpec(memory_space=pl.ANY)
    dma = pltpu.SemaphoreType.DMA
    n = fsdp_count
    i16 = jnp.int16
    return pl.pallas_call(
        functools.partial(reduce_kernel, seq_count, fsdp_count),
        out_shape=(
            jax.ShapeDtypeStruct((seq_count, final, columns), F32),
            jax.ShapeDtypeStruct((max(seq_count - 1, 1), local, features), BF16),
            jax.ShapeDtypeStruct((local, seq_count * gw), BF16),
        ),
        in_specs=[vmem, vmem, any_spec, any_spec],
        out_specs=(vmem, any_spec, any_spec),
        scratch_shapes=[
            pltpu.VMEM((2 * n, rows, columns), F32),
            pltpu.VMEM((2 * n, rows, columns), F32),
            pltpu.VMEM((n, rows, columns), i16),
            pltpu.VMEM((n, rows, columns), i16),
            pltpu.VMEM((n, 1, columns), F32),
            pltpu.VMEM((n, 1, columns), F32),
            pltpu.VMEM((n, rows, columns), i16),
            pltpu.VMEM((n, rows, columns), i16),
            pltpu.VMEM((n, 1, columns), F32),
            pltpu.VMEM((n, 1, columns), F32),
            pltpu.VMEM((rows, columns), F32),
            pltpu.VMEM((seq_count, final, columns), F32),
            dma,
        ]
        + [dma((2 * n,))] * 2
        + [dma((n,))] * 8
        + [dma((seq_count,))] * 6,
        compiler_params=pltpu.CompilerParams(
            collective_id=1, has_side_effects=True, vmem_limit_bytes=VMEM_BYTES
        ),
        name="reduce_gradients",
    )(normed_t, grad, dx, ctx)


def standardise(rows):
    as_float = rows.astype(F32)
    centered = as_float - jnp.mean(as_float, axis=1, keepdims=True)
    inv_std = lax.rsqrt(jnp.mean(centered * centered, axis=1, keepdims=True) + EPS)
    return centered * inv_std, inv_std


def body(frames, projection, lengths, cotangent):
    inputs = frames[0]
    upstream = cotangent[0]
    seq_count = lax.axis_size("seq")
    fsdp_count = lax.axis_size("fsdp")
    me = lax.axis_index("seq")
    local, features = inputs.shape
    gw = HEADS // seq_count * HD
    w_mine = lax.dynamic_index_in_dim(
        projection.reshape(-1, 3, seq_count, gw), me, axis=2, keepdims=False
    ).reshape(-1, 3 * gw)
    w_all, x_all, c_all = gather(w_mine, inputs, upstream, seq_count, fsdp_count, gw)
    normed = standardise(x_all)[0].astype(BF16)
    packed = jnp.dot(normed, w_all, preferred_element_type=F32).astype(BF16)
    ctx, grad = attention(lengths, packed, c_all, gw)
    partial = nt(grad, w_all)
    out, dx, context = reduce(
        normed.T, grad, partial.astype(BF16), ctx, seq_count, fsdp_count, local
    )
    normed_gradient = lax.dynamic_slice_in_dim(partial, me * local, local, 0)
    for d in range(seq_count - 1):
        normed_gradient = normed_gradient + dx[d].astype(F32)
    standard, inv_std = standardise(inputs)
    row_mean = jnp.mean(normed_gradient, axis=1, keepdims=True)
    projected = jnp.mean(normed_gradient * standard, axis=1, keepdims=True)
    input_gradient = inv_std * (normed_gradient - row_mean - standard * projected)
    projection_gradient = (
        out.reshape(seq_count, -1, 3, gw).transpose(1, 2, 0, 3).reshape(-1, 3 * seq_count * gw)
    )
    return (context[None], input_gradient[None], projection_gradient)


def solution(mesh):
    placed = (
        P(("dp", "fsdp"), "seq", None),
        P("fsdp", None),
        P(("dp", "fsdp")),
        P(("dp", "fsdp"), "seq", None),
    )
    return jax.shard_map(
        body,
        mesh=mesh,
        in_specs=placed,
        out_specs=(
            P(("dp", "fsdp"), "seq", None),
            P(("dp", "fsdp"), "seq", None),
            P(("dp", "fsdp", "seq"), None),
        ),
        check_vma=False,
    )
```

```python
import functools
import math

import jax
import jax.numpy as jnp
from jax import lax
from jax.experimental import pallas as pl
from jax.experimental.pallas import tpu as pltpu
from jax.sharding import PartitionSpec as P

HEADS = 16
HD = 64
EPS = 1e-05
MESH = pl.DeviceIdType.MESH
F32 = jnp.float32
BF16 = jnp.bfloat16
VMEM_BYTES = 56 * 1024 * 1024


def ring(axis, step):
    size = lax.axis_size(axis)
    return lax.rem(lax.axis_index(axis) + step + size, size)


def greet(seq_count, fsdp_count, dp):
    barrier = pltpu.get_barrier_semaphore()
    for peer in (dp ^ 1, dp ^ 2):
        pl.semaphore_signal(barrier, inc=1, device_id={"dp": peer}, device_id_type=MESH)
    for d in range(1, fsdp_count):
        pl.semaphore_signal(barrier, inc=1, device_id={"fsdp": ring("fsdp", d)}, device_id_type=MESH)
    for d in range(1, seq_count):
        pl.semaphore_signal(barrier, inc=1, device_id={"seq": ring("seq", d)}, device_id_type=MESH)
    pl.semaphore_wait(barrier, 2 + fsdp_count - 1 + seq_count - 1)


def gather_kernel(
    seq_count, n, w_ref, x_ref, c_ref, w_all, x_all, c_all,
    local_sem, xs, xr, cs, cr, zs, zr, f1s, f1r, f2s, f2r, f3s, f3r,
):
    dp = lax.axis_index("dp")
    fs = lax.axis_index("fsdp")
    me = lax.axis_index("seq")
    rows = w_ref.shape[0]
    quarter = rows // 4
    local = x_ref.shape[0]
    gw = c_all.shape[1]
    block_rows = pl.ds(pl.multiple_of(fs * rows, 16), rows)
    picks = []
    for kind in range(3):
        column = pl.multiple_of((kind * seq_count + me) * gw, 128)
        picks.append(
            pltpu.make_async_copy(
                w_ref.at[:, pl.ds(column, gw)],
                w_all.at[block_rows, pl.ds(kind * gw, gw)],
                local_sem.at[kind],
            )
        )
    for copy in picks:
        copy.start()
    greet(seq_count, n, dp)

    def part(block, q):
        return w_all.at[pl.ds(pl.multiple_of(block * rows + q * quarter, 16), quarter)]

    def remote(src, dst, send, recv, where):
        return pltpu.make_async_remote_copy(
            src_ref=src, dst_ref=dst, send_sem=send, recv_sem=recv, device_id=where, device_id_type=MESH
        )

    def along(block, index, up):
        peer = ring("fsdp", 1 if up else -1)
        return remote(part(block, dp), part(block, dp), zs.at[index], zr.at[index], {"fsdp": peer})

    def forward1(block, index):
        return remote(part(block, dp), part(block, dp), f1s.at[index], f1r.at[index], {"dp": dp ^ 1})

    def forward2(block, index):
        return remote(part(block, dp), part(block, dp), f2s.at[index], f2r.at[index], {"dp": dp ^ 2})

    def forward3(block, index):
        other = part(block, dp ^ 2)
        return remote(other, other, f3s.at[index], f3r.at[index], {"dp": dp ^ 1})

    for copy in picks:
        copy.wait()

    @pl.when(fs < n - 1)
    def _():
        along(fs, 1, True).start()

    @pl.when(fs > 0)
    def _():
        along(fs, n + 1, False).start()

    here = pl.ds(pl.multiple_of(me * local, 16), local)
    seq_copies = []
    for d in range(1, seq_count):
        peer = ring("seq", d)
        a = remote(x_ref, x_all.at[here], xs.at[d], xr.at[d], {"seq": peer})
        b = remote(
            c_ref.at[:, pl.ds(pl.multiple_of(peer * gw, 128), gw)],
            c_all.at[here], cs.at[d], cr.at[d], {"seq": peer},
        )
        a.start()
        b.start()
        seq_copies += [a, b]
    x_all[here, :] = x_ref[...]
    c_all[here, :] = c_ref[:, pl.ds(pl.multiple_of(me * gw, 128), gw)]

    def each(act):
        for t in range(1, n):
            for up in (True, False):
                block = fs - t if up else fs + t
                exists = (block >= 0) & (block <= n - 1)
                index = t if up else n + t

                @pl.when(exists)
                def _():
                    act(block, index, up)

    def goes_on(up):
        return fs < n - 1 if up else fs > 0

    def take(block, index, up):
        along(block, index, up).wait_recv()

        @pl.when(goes_on(up))
        def _():
            along(block, index + 1, up).start()

        forward2(block, index).start()
        forward1(block, index).start()

    def pass_on(block, index, up):
        forward2(block, index).wait_recv()
        forward3(block, index).start()

    def finish(block, index, up):
        forward1(block, index).wait_recv()
        forward3(block, index).wait_recv()

    def drain(block, index, up):
        @pl.when(goes_on(up))
        def _():
            along(block, index + 1, up).wait_send()

        forward1(block, index).wait_send()
        forward2(block, index).wait_send()
        forward3(block, index).wait_send()

    each(take)
    each(pass_on)
    each(finish)
    for copy in seq_copies:
        copy.wait()
    each(drain)

    @pl.when(fs < n - 1)
    def _():
        along(fs, 1, True).wait_send()

    @pl.when(fs > 0)
    def _():
        along(fs, n + 1, False).wait_send()


def gather(w, x, c, seq_count, fsdp_count, gw):
    any_spec = pl.BlockSpec(memory_space=pl.ANY)
    vmem = pl.BlockSpec(memory_space=pltpu.VMEM)
    dma = pltpu.SemaphoreType.DMA
    total = x.shape[0] * seq_count
    return pl.pallas_call(
        functools.partial(gather_kernel, seq_count, fsdp_count),
        out_shape=(
            jax.ShapeDtypeStruct((w.shape[0] * fsdp_count, 3 * gw), BF16),
            jax.ShapeDtypeStruct((total, x.shape[1]), BF16),
            jax.ShapeDtypeStruct((total, gw), BF16),
        ),
        in_specs=[any_spec, vmem, vmem],
        out_specs=(vmem,) * 3,
        scratch_shapes=[dma((3,))] + [dma((seq_count,))] * 4 + [dma((2 * fsdp_count + 1,))] * 8,
        compiler_params=pltpu.CompilerParams(
            collective_id=0, has_side_effects=True, vmem_limit_bytes=VMEM_BYTES
        ),
        name="gather_inputs",
    )(w, x, c)


def nt(a, b):
    return lax.dot_general(a, b, (((1,), (1,)), ((), ())), preferred_element_type=F32)


def tn(a, b):
    return lax.dot_general(a, b, (((0,), (0,)), ((), ())), preferred_element_type=F32)


def attention_kernel(len_ref, q_ref, k_ref, v_ref, o_ref, ctx_ref, grad_ref, dk_acc, dv_acc):
    pair = pl.program_id(0)
    step = pl.program_id(1)
    steps = pl.num_programs(1)
    length = len_ref[0]
    block, width = q_ref.shape
    keys = k_ref.shape[0]
    gw = grad_ref.shape[1] // 3
    factor = 1.0 / math.sqrt(HD)
    key_ok = lax.broadcasted_iota(jnp.int32, (keys, block), 0) < length
    row = lax.broadcasted_iota(jnp.int32, (block, width), 0) + step * block
    row_ok = row < length
    k, v, q = k_ref[...], v_ref[...], q_ref[...]
    upstream = jnp.where(row_ok, o_ref[...], jnp.zeros_like(o_ref[...]))
    key_lane = lax.broadcasted_iota(jnp.int32, (keys, width), 1)
    row_lane = lax.broadcasted_iota(jnp.int32, (block, width), 1)

    @pl.when(step == 0)
    def _():
        dk_acc[...] = jnp.zeros_like(dk_acc)
        dv_acc[...] = jnp.zeros_like(dv_acc)

    context_t = jnp.zeros((width, block), F32)
    query_t = jnp.zeros((width, block), F32)
    dk = dk_acc[...]
    dv = dv_acc[...]
    for head in range(width // HD):
        low, high = head * HD, (head + 1) * HD
        on_key = (key_lane >= low) & (key_lane < high)
        on_row = (row_lane >= low) & (row_lane < high)
        k_h = jnp.where(on_key, k, jnp.zeros_like(k))
        v_h = jnp.where(on_key, v, jnp.zeros_like(v))
        q_h = jnp.where(on_row, q, jnp.zeros_like(q))
        o_h = jnp.where(on_row, upstream, jnp.zeros_like(upstream))
        scores = jnp.where(key_ok, nt(k_h, q), -jnp.inf)
        peak = jnp.max(scores, axis=0, keepdims=True)
        e = jnp.exp((scores - peak) * factor)
        p = e * (1.0 / jnp.sum(e, axis=0, keepdims=True))
        weights = p.astype(BF16)
        context_t += tn(v_h, weights)
        dv += jnp.dot(weights, o_h, preferred_element_type=F32)
        dp = nt(v_h, upstream)
        inner = jnp.sum(p * dp, axis=0, keepdims=True)
        ds = (p * (dp - inner) * factor).astype(BF16)
        query_t += tn(k_h, ds)
        dk += jnp.dot(ds, q_h, preferred_element_type=F32)
    context = context_t.T
    ctx_ref[...] = jnp.where(row_ok, context, jnp.zeros_like(context)).astype(BF16)
    rows = pl.ds(pl.multiple_of(step * block, block), block)
    column = pl.multiple_of(pair * width, width)
    grad_ref[rows, pl.ds(column, width)] = query_t.T.astype(BF16)
    dk_acc[...] = dk
    dv_acc[...] = dv

    @pl.when(step == steps - 1)
    def _():
        grad_ref[:, pl.ds(pl.multiple_of(gw + column, width), width)] = dk.astype(BF16)
        grad_ref[:, pl.ds(pl.multiple_of(2 * gw + column, width), width)] = dv.astype(BF16)


def attention(length, packed, c_all, gw):
    total = packed.shape[0]
    block = min(total, 512)
    width = 2 * HD
    pairs = gw // width
    return pl.pallas_call(
        attention_kernel,
        grid=(pairs, total // block),
        out_shape=(
            jax.ShapeDtypeStruct((total, gw), BF16),
            jax.ShapeDtypeStruct((total, 3 * gw), BF16),
        ),
        in_specs=[
            pl.BlockSpec(memory_space=pltpu.SMEM),
            pl.BlockSpec((block, width), lambda h, i: (i, h)),
            pl.BlockSpec((total, width), lambda h, i: (0, pairs + h)),
            pl.BlockSpec((total, width), lambda h, i: (0, 2 * pairs + h)),
            pl.BlockSpec((block, width), lambda h, i: (i, h)),
        ],
        out_specs=(
            pl.BlockSpec((block, width), lambda h, i: (i, h)),
            pl.BlockSpec((total, 3 * gw), lambda h, i: (0, 0)),
        ),
        scratch_shapes=[pltpu.VMEM((total, width), F32)] * 2,
        compiler_params=pltpu.CompilerParams(vmem_limit_bytes=VMEM_BYTES),
        cost_estimate=pl.CostEstimate(
            flops=12 * total * total * gw, bytes_accessed=16 * total * gw, transcendentals=total * total * gw // HD
        ),
        name="attention",
    )(length, packed, packed, packed, c_all)


def encode(value):
    peak = jnp.maximum(jnp.max(jnp.abs(value), axis=0, keepdims=True), 1e-30)
    code = jnp.round(value * (32767.0 / peak)).astype(jnp.int32).astype(jnp.int16)
    return code, peak * (1.0 / 32767.0)


def decode(code, scale):
    return code.astype(jnp.int32).astype(F32) * scale


def reduce_kernel(
    seq_count, fsdp_count, nt_ref, grad_ref, w_ref, frames_ref, ctx_ref, out_ref, input_out, ctx_out,
    s1, r1, s2, r2, t2, u2, s3, r3, t3, u3, total, s4, r4, sdx, rdx, normed_gradient,
    local_sem, s1s, s1r, s2s, s2r, t2s, t2r, s3s, s3r, t3s, t3r, s4s, s4r, xs, xr, cs, cr,
):
    dp = lax.axis_index("dp")
    fs = lax.axis_index("fsdp")
    me = lax.axis_index("seq")
    features = nt_ref.shape[0]
    rows = features // (4 * fsdp_count)
    local = frames_ref.shape[0]
    gw = ctx_ref.shape[1]
    final = rows // seq_count
    greet(seq_count, fsdp_count, dp)

    def remote(src, dst, send, recv, where):
        return pltpu.make_async_remote_copy(
            src_ref=src, dst_ref=dst, send_sem=send, recv_sem=recv, device_id=where, device_id_type=MESH
        )

    mine_columns = pl.ds(pl.multiple_of(me * gw, 128), gw)
    seq_copies = []
    for d in range(1, seq_count):
        peer = ring("seq", d)
        there = pl.ds(pl.multiple_of(peer * local, 16), local)
        copy = remote(ctx_ref.at[there], ctx_out.at[:, mine_columns], cs.at[d], cr.at[d], {"seq": peer})
        seq_copies.append(copy)
    own = pltpu.make_async_copy(
        ctx_ref.at[pl.ds(pl.multiple_of(me * local, 16), local)], ctx_out.at[:, mine_columns], local_sem
    )
    for copy in seq_copies:
        copy.start()
    own.start()

    def product(block, step):
        sub = lax.rem(fs + 1 + step, fsdp_count)
        start = pl.multiple_of(block * (rows * fsdp_count) + sub * rows, 16)
        return jnp.dot(nt_ref[pl.ds(start, rows), :], grad_ref[...], preferred_element_type=F32)

    core = lax.rem(dp, 2)
    far = 2 * (1 - dp // 2)
    near = 2 * (dp // 2)

    def copy1(i):
        return remote(s1.at[i], r1.at[i], s1s.at[i], s1r.at[i], {"dp": dp ^ 1})

    def copy2(d):
        return (
            remote(s2.at[d], r2.at[d], s2s.at[d], s2r.at[d], {"dp": dp ^ 2}),
            remote(t2.at[d], u2.at[d], t2s.at[d], t2r.at[d], {"dp": dp ^ 2}),
        )

    def copy3(d):
        peer = lax.rem(fs + 1 + d, fsdp_count)
        return (
            remote(s3.at[d], r3.at[d], s3s.at[d], s3r.at[d], {"fsdp": peer}),
            remote(t3.at[d], u3.at[d], t3s.at[d], t3r.at[d], {"fsdp": peer}),
        )

    def loop(count, body):
        lax.fori_loop(0, count, lambda i, _: (body(i), 0)[1], 0)

    def to_core(i):
        block = jnp.where(i < fsdp_count, far, near) + (1 - core)
        s1[i] = product(block, lax.rem(i, fsdp_count))
        copy1(i).start()

    def feature_gradient(peer):
        part = grad_ref[pl.ds(pl.multiple_of(peer * local, 16), local), :]
        return nt(part, w_ref[...])

    def copy_dx(d):
        peer = lax.rem(me + d, seq_count)
        return remote(sdx.at[d - 1], rdx.at[d - 1], xs.at[d], xr.at[d], {"seq": peer})

    def to_seq(i):
        d = i + 1
        sdx[i] = feature_gradient(lax.rem(me + d, seq_count)).astype(BF16)
        copy_dx(d).start()

    loop(2 * fsdp_count, to_core)
    loop(seq_count - 1, to_seq)

    def to_x(d):
        own_part = product(far + core, d)
        copy1(d).wait_recv()
        code, scale = encode(own_part + r1[d])
        s2[d] = code
        t2[d] = scale
        for copy in copy2(d):
            copy.start()

    loop(fsdp_count, to_x)
    normed_gradient[...] = feature_gradient(me)

    def arrived(d):
        own_part = product(near + core, d)
        copy1(fsdp_count + d).wait_recv()
        for copy in copy2(d):
            copy.wait_recv()
        return own_part + r1[fsdp_count + d] + decode(r2[d], u2[d])

    def to_z(d):
        code, scale = encode(arrived(d))
        s3[d] = code
        t3[d] = scale
        for copy in copy3(d):
            copy.start()

    loop(fsdp_count - 1, to_z)
    total[...] = arrived(fsdp_count - 1)

    def add_z(d):
        for copy in copy3(d):
            copy.wait_recv()
        total[...] += decode(r3[d], u3[d])

    loop(fsdp_count - 1, add_z)
    for p in range(seq_count):
        s4[p] = total[p * final : (p + 1) * final, :]
    last = []
    for d in range(1, seq_count):
        peer = ring("seq", d)
        copy = remote(s4.at[peer], r4.at[me], s4s.at[d], s4r.at[d], {"seq": peer})
        copy.start()
        last.append(copy)
    r4[me] = s4[me]

    def from_seq(i):
        copy_dx(i + 1).wait_recv()
        normed_gradient[...] += rdx[i].astype(F32)

    loop(seq_count - 1, from_seq)
    gradient = normed_gradient[...]
    standard, inv_std = standardise(frames_ref[...])
    row_mean = jnp.mean(gradient, axis=1, keepdims=True)
    projected = jnp.mean(gradient * standard, axis=1, keepdims=True)
    input_out[...] = inv_std * (gradient - row_mean - standard * projected)
    for copy in last:
        copy.wait()
    for p in range(seq_count):
        for kind in range(3):
            column = (kind * seq_count + p) * gw
            out_ref[:, column : column + gw] = r4[p, :, kind * gw : (kind + 1) * gw]
    for copy in seq_copies:
        copy.wait()
    own.wait()

    def drain1(i):
        copy1(i).wait_send()

    def drain2(d):
        for copy in copy2(d):
            copy.wait_send()

    def drain3(d):
        for copy in copy3(d):
            copy.wait_send()

    def drain_dx(i):
        copy_dx(i + 1).wait_send()

    loop(seq_count - 1, drain_dx)
    loop(2 * fsdp_count, drain1)
    loop(fsdp_count, drain2)
    loop(fsdp_count - 1, drain3)


def reduce(normed_t, grad, w_all, frames, ctx, seq_count, fsdp_count):
    local = frames.shape[0]
    features, columns = normed_t.shape[0], grad.shape[1]
    gw = columns // 3
    rows = features // (4 * fsdp_count)
    final = rows // seq_count
    vmem = pl.BlockSpec(memory_space=pltpu.VMEM)
    any_spec = pl.BlockSpec(memory_space=pl.ANY)
    dma = pltpu.SemaphoreType.DMA
    n = fsdp_count
    i16 = jnp.int16
    return pl.pallas_call(
        functools.partial(reduce_kernel, seq_count, fsdp_count),
        out_shape=(
            jax.ShapeDtypeStruct((final, seq_count * columns), F32),
            jax.ShapeDtypeStruct((local, features), F32),
            jax.ShapeDtypeStruct((local, seq_count * gw), BF16),
        ),
        in_specs=[vmem, vmem, vmem, vmem, any_spec],
        out_specs=(vmem, vmem, any_spec),
        scratch_shapes=[
            pltpu.VMEM((2 * n, rows, columns), F32),
            pltpu.VMEM((2 * n, rows, columns), F32),
            pltpu.VMEM((n, rows, columns), i16),
            pltpu.VMEM((n, rows, columns), i16),
            pltpu.VMEM((n, 1, columns), F32),
            pltpu.VMEM((n, 1, columns), F32),
            pltpu.VMEM((n, rows, columns), i16),
            pltpu.VMEM((n, rows, columns), i16),
            pltpu.VMEM((n, 1, columns), F32),
            pltpu.VMEM((n, 1, columns), F32),
            pltpu.VMEM((rows, columns), F32),
            pltpu.VMEM((seq_count, final, columns), F32),
            pltpu.VMEM((seq_count, final, columns), F32),
            pltpu.VMEM((seq_count - 1, local, features), BF16),
            pltpu.VMEM((seq_count - 1, local, features), BF16),
            pltpu.VMEM((local, features), F32),
            dma,
        ]
        + [dma((2 * n,))] * 2
        + [dma((n,))] * 8
        + [dma((seq_count,))] * 6,
        compiler_params=pltpu.CompilerParams(
            collective_id=1, has_side_effects=True, vmem_limit_bytes=VMEM_BYTES
        ),
        name="reduce_gradients",
    )(normed_t, grad, w_all, frames, ctx)


def standardise(rows):
    as_float = rows.astype(F32)
    centered = as_float - jnp.mean(as_float, axis=1, keepdims=True)
    inv_std = lax.rsqrt(jnp.mean(centered * centered, axis=1, keepdims=True) + EPS)
    return centered * inv_std, inv_std


def body(frames, projection, lengths, cotangent):
    inputs = frames[0]
    upstream = cotangent[0]
    seq_count = lax.axis_size("seq")
    fsdp_count = lax.axis_size("fsdp")
    gw = HEADS // seq_count * HD
    normed_mine = standardise(inputs)[0].astype(BF16)
    w_all, normed, c_all = gather(projection, normed_mine, upstream, seq_count, fsdp_count, gw)
    packed = jnp.dot(normed, w_all, preferred_element_type=F32).astype(BF16)
    ctx, grad = attention(lengths, packed, c_all, gw)
    projection_gradient, input_gradient, context = reduce(
        normed.T, grad, w_all, inputs, ctx, seq_count, fsdp_count
    )
    return (context[None], input_gradient[None], projection_gradient)


def solution(mesh):
    placed = (
        P(("dp", "fsdp"), "seq", None),
        P("fsdp", None),
        P(("dp", "fsdp")),
        P(("dp", "fsdp"), "seq", None),
    )
    return jax.shard_map(
        body,
        mesh=mesh,
        in_specs=placed,
        out_specs=(
            P(("dp", "fsdp"), "seq", None),
            P(("dp", "fsdp"), "seq", None),
            P(("dp", "fsdp", "seq"), None),
        ),
        check_vma=False,
    )
```
